1024 devices in a mesh: expert: 32 (over z), dp: 32 (over x, y, core).
Axes of the slice: x: 4, y: 4, z: 32, core: 2. Of those that a mesh axis runs over, the one named last changes fastest.
Arguments:
- tokens: bfloat16 [8192, 4096], P('dp'), may hold values from -6 to 6
- out_grad: bfloat16 [8192, 4096], P('dp'), may hold values from -6 to 6
- expert_ids: int32 [8192, 8], P('dp'), may hold values from 0 to 63, all different within a row
- gate_fixed: int32 [8192, 8], P('dp'), may hold values from 1 to 65535
- expert_pick: int32 [1], replicated, may hold values from 0 to 63
- w_gate: bfloat16 [64, 4096, 1024], P('expert', 'dp'), may hold values from -0.09375 to 0.09375
- w_up: bfloat16 [64, 4096, 1024], P('expert', 'dp'), may hold values from -0.09375 to 0.09375
- w_down: bfloat16 [64, 4096, 1024], P('expert', 'dp'), may hold values from -0.1875 to 0.1875
Outputs:
- moe_out: bfloat16 [8192, 4096], P('dp', 'expert')
- token_grad: bfloat16 [8192, 4096], P('dp', 'expert')
- grad_gate: bfloat16 [64, 4096, 1024], P('expert', 'dp')
- grad_up: bfloat16 [64, 4096, 1024], P('expert', 'dp')
- grad_down: bfloat16 [64, 4096, 1024], P('expert', 'dp')
The draws below stay inside these ranges and needn't reach their ends.
Inputs may be any that keep to these rules, and one draw needn't show every extreme that they name: `expert_ids`: each row names 8 different experts.
All inputs are finite; a program needn't handle non-finite values.
Results may differ from the reference program's by a relative error of at most 0.023.
Values may be sent and summed in bfloat16 or wider, within the bound.
A program may use at most 32 MiB of HBM per device.

```python
import jax
import jax.numpy as jnp
from jax import lax

D = 4096
F = 1024
E = 64
TOPK = 8
TOKENS = 8192
BLOCKS = 8
HB = 128
REPL = 4
TR = 64
N_DP = 32


def plant(drawn, key, low, high):
    longest = drawn.shape.index(max(drawn.shape))
    spots = []
    for shift in (0, 1):
        where = [jax.random.randint(jax.random.fold_in(key, axis), (), 0, length) for axis, length in enumerate(drawn.shape)]
        where[longest] = (where[longest] + shift) % drawn.shape[longest]
        spots.append(tuple(where))
    return drawn.at[spots[0]].set(low).at[spots[1]].set(high)


def steps_of(own_key, shape, split, low, largest):
    factor_of, own = 1.0, jax.random.fold_in(own_key, 6)
    for dim, blocks in split:
        draws = jnp.exp(jax.random.uniform(jax.random.fold_in(own, dim), (blocks,), jnp.float32, low / len(split), largest / len(split)))
        factor_of = factor_of * jnp.repeat(draws, shape[dim] // blocks).reshape([-1 if axis == dim else 1 for axis in range(len(shape))])
    return factor_of


def different_ones(key, rows, count, top, lift):
    ranking = jax.random.permutation(jax.random.fold_in(key, 1), count)
    favour = ranking
    for power in range(3):
        favour = favour * favour // count
    favour = favour * lift // count
    chance = jax.random.randint(jax.random.fold_in(key, 2), (rows, count), 0, 4096) + favour
    sure = jax.random.permutation(jax.random.fold_in(key, 3), rows)[jnp.arange(count) % rows]
    chance = jnp.where(jnp.arange(rows)[:, None] == sure[None, :], 1 << 14, chance)
    merit = chance * count + jnp.arange(count)
    return lax.top_k(merit.astype(jnp.int32), top)[1].astype(jnp.int32)


def centred(stream_key, dims, width, limit, pieces=(), dtype=jnp.bfloat16):
    values = jax.random.normal(stream_key, dims, jnp.float32) * width
    if len(pieces) > 0:
        values = steps_of(stream_key, dims, pieces, -0.22, 0.18) * values
    return jnp.clip(values, min=-limit, max=limit).astype(dtype)


def setup_inputs(seed: int = 0) -> dict:
    keys = jax.random.split(jax.random.key(seed), 9)
    tokens = centred(keys[0], (TOKENS, D), 1.0, 6.0, ((0, 32),))
    out_grad = centred(keys[1], (TOKENS, D), 1.0, 6.0, ((0, 32),))
    expert_ids = different_ones(keys[2], TOKENS, E, TOPK, 2048)
    gate_fixed = plant(jax.random.randint(keys[3], (TOKENS, TOPK), 1, 65536), jax.random.fold_in(keys[3], 1), 1, 65535).astype(jnp.int32)
    expert_pick = jax.random.randint(keys[4], (1,), 0, E).astype(jnp.int32)
    w_gate = centred(keys[5], (E, D, F), D ** -0.5, 0.09375, ((0, 32), (1, 32)))
    w_up = centred(keys[6], (E, D, F), D ** -0.5, 0.09375, ((0, 32), (1, 32)))
    w_down = centred(keys[7], (E, D, F), F ** -0.5, 0.1875, ((0, 32), (1, 32)))
    return {"tokens": tokens, "out_grad": out_grad, "expert_ids": expert_ids, "gate_fixed": gate_fixed, "expert_pick": expert_pick, "w_gate": w_gate, "w_up": w_up, "w_down": w_down}


def combine_weight(expert_ids, gate_fixed, picked):
    matched = jnp.where(expert_ids == picked, gate_fixed, 0)
    return (lax.optimization_barrier(jnp.sum(matched, axis=1)).astype(jnp.float32) / 65536.0)[:, None]

def round_trip(values):
    return lax.optimization_barrier(values.astype(jnp.bfloat16)).astype(jnp.float32)

def quarter_grads(left_side, right_side):

    def add_one(running, operands):
        product = lax.dot_general(operands[0], operands[1], (((0,), (0,)), ((), ())), preferred_element_type=jnp.float32)
        return (running + round_trip(product), None)
    initial = jnp.zeros((left_side.shape[2], right_side.shape[2]), jnp.float32)
    running, unused = lax.scan(add_one, initial, (left_side, right_side))
    return running

def weight_grad(left_side, right_side):
    left_split = left_side.reshape(N_DP, REPL, TR, left_side.shape[1])
    right_split = right_side.reshape(N_DP, REPL, TR, right_side.shape[1])
    running = jnp.zeros((left_side.shape[1], right_side.shape[1]), jnp.float32)
    for quarter in range(REPL):
        running = running + round_trip(quarter_grads(left_split[:, quarter], right_split[:, quarter]))
    return running.astype(jnp.bfloat16)

def reference(tokens, out_grad, expert_ids, gate_fixed, expert_pick, w_gate, w_up, w_down):
    picked = expert_pick[0].astype(jnp.int32)
    weight = combine_weight(expert_ids, gate_fixed, picked)
    gate_mat = lax.dynamic_index_in_dim(w_gate, picked, 0, keepdims=False)
    up_mat = lax.dynamic_index_in_dim(w_up, picked, 0, keepdims=False)
    down_mat = lax.dynamic_index_in_dim(w_down, picked, 0, keepdims=False)
    gate_val = jnp.dot(tokens, gate_mat, preferred_element_type=jnp.float32)
    up_val = jnp.dot(tokens, up_mat, preferred_element_type=jnp.float32)
    sigmoid_gate = jax.nn.sigmoid(gate_val)
    activated = gate_val * sigmoid_gate
    hidden = (weight * activated * up_val).astype(jnp.bfloat16)
    hidden_grad = jnp.dot(out_grad, down_mat, preferred_element_type=jnp.float32)
    d_gate = (weight * hidden_grad * up_val * sigmoid_gate * (1.0 + gate_val * (1.0 - sigmoid_gate))).astype(jnp.bfloat16)
    d_up = (weight * hidden_grad * activated).astype(jnp.bfloat16)
    contract = (((1,), (1,)), ((), ()))
    moe_sum = jnp.zeros(tokens.shape, jnp.float32)
    input_grad = jnp.zeros(tokens.shape, jnp.float32)
    for block_number in range(BLOCKS):
        lower = block_number * HB
        upper = lower + HB
        partial_value = lax.dot_general(hidden[:, lower:upper], down_mat[:, lower:upper], contract, preferred_element_type=jnp.float32)
        moe_sum = moe_sum + round_trip(partial_value)
        partial_dx = lax.dot_general(d_gate[:, lower:upper], gate_mat[:, lower:upper], contract, preferred_element_type=jnp.float32)
        partial_dx = partial_dx + lax.dot_general(d_up[:, lower:upper], up_mat[:, lower:upper], contract, preferred_element_type=jnp.float32)
        input_grad = input_grad + round_trip(partial_dx)
    grad_gate = lax.dynamic_update_index_in_dim(jnp.zeros_like(w_gate), weight_grad(tokens, d_gate), picked, 0)
    grad_up = lax.dynamic_update_index_in_dim(jnp.zeros_like(w_up), weight_grad(tokens, d_up), picked, 0)
    grad_down = lax.dynamic_update_index_in_dim(jnp.zeros_like(w_down), weight_grad(out_grad, hidden), picked, 0)
    return (moe_sum.astype(jnp.bfloat16), input_grad.astype(jnp.bfloat16), grad_gate, grad_up, grad_down)
```

```python
import functools

import jax
import jax.numpy as jnp
from jax import lax
from jax.experimental import pallas as pl
from jax.experimental.pallas import tpu as pltpu
from jax.sharding import PartitionSpec as P

NZ, ND = 32, 32
K, FQ = 8, 4
STRIP, HQ, PIECE = 128, 256, 16
WIDTH = FQ * STRIP
MESH = pl.DeviceIdType.MESH
BF = jnp.bfloat16
F32 = jnp.float32
LIMIT = 48 << 20
VM = pl.BlockSpec(memory_space=pltpu.VMEM)
HBM = pl.BlockSpec(memory_space=pl.ANY)
SM = pl.BlockSpec(memory_space=pltpu.SMEM)


def place():
    z = lax.axis_index("expert")
    d = lax.axis_index("dp")
    return z, d, lax.div(z, K), lax.rem(z, K)


def greet(barrier, device):
    pl.semaphore_signal(barrier, inc=1, device_id=device, device_id_type=MESH)


def remote(src, dst, send, recv, device):
    return pltpu.make_async_remote_copy(
        src_ref=src, dst_ref=dst, send_sem=send, recv_sem=recv, device_id=device, device_id_type=MESH
    )


def at_chip(d, shift):
    chip, core = lax.div(d, 2), lax.rem(d, 2)
    return lax.rem(chip + shift, 16) * 2 + core


def twin(d):
    return d + 1 - 2 * lax.rem(d, 2)


def greet_plane(barrier, z, d):
    @pl.loop(1, 16)
    def _(shift):
        greet(barrier, (z, at_chip(d, shift)))

    greet(barrier, (z, twin(d)))


def nn(a, b):
    return jnp.dot(a, b, preferred_element_type=F32)


def nt(a, b):
    return lax.dot_general(a, b, (((1,), (1,)), ((), ())), preferred_element_type=F32)


def tn(a, b):
    return lax.dot_general(a, b, (((0,), (0,)), ((), ())), preferred_element_type=F32)


def pull_kernel(z0, pick, wg, wu, wd, brick, both, stage, load, piece_send, piece_recv, go_send, go_recv, twin_send, twin_recv):
    z, d, f, k = place()
    f0, k0 = z0 // K, z0 % K
    here = jnp.logical_and(z == z0, lax.rem(d, K) == k0)
    source = lax.div(d, K) * K + k
    barrier = pltpu.get_barrier_semaphore()
    greet_plane(barrier, z, d)

    @pl.when(jnp.logical_not(here))
    def _():
        greet(barrier, (z0, source))

    mine = pl.ds(pl.multiple_of(d * PIECE, PIECE), PIECE)

    @pl.when(z == z0)
    def _():
        loads = [pltpu.make_async_copy(w, both.at[m], load.at[m]) for m, w in enumerate((wg, wu, wd))]
        for copy in loads:
            copy.start()
        for copy in loads:
            copy.wait()
        slot = lax.rem(pick[0], 2)
        for m in range(3):
            stage[m] = jnp.where(slot == 0, both[m, 0], both[m, 1])

        def target(i):
            return lax.div(i, K) * K + lax.rem(d, K), lax.div(d, K) * K + lax.rem(i, K)

        def away(i):
            to_z, to_d = target(i)
            return jnp.logical_or(to_z != z, to_d != d)

        def give(i):
            to_z, to_d = target(i)
            rows = pl.ds(pl.multiple_of(lax.rem(i, K) * PIECE, PIECE), PIECE)
            cols = pl.ds(pl.multiple_of(lax.div(i, K) * HQ, HQ), HQ)
            there = pl.ds(pl.multiple_of(to_d * PIECE, PIECE), PIECE)
            return remote(
                stage.at[:, rows, cols], brick.at[:, there, :], piece_send.at[i], piece_recv, (to_z, to_d)
            )

        @pl.when(here)
        def _():
            pl.semaphore_wait(barrier, 31 + 16)

        @pl.when(jnp.logical_not(here))
        def _():
            pl.semaphore_wait(barrier, 32 + 16)

        @pl.loop(0, 32)
        def _(i):
            @pl.when(away(i))
            def _():
                give(i).start()

        @pl.when(here)
        def _():
            own = pltpu.make_async_copy(
                stage.at[:, pl.ds(k0 * PIECE, PIECE), pl.ds(f0 * HQ, HQ)], brick.at[:, mine, :], load.at[3]
            )
            own.start()
            own.wait()

        @pl.loop(0, 32)
        def _(i):
            @pl.when(away(i))
            def _():
                give(i).wait_send()

    @pl.when(z != z0)
    def _():
        pl.semaphore_wait(barrier, 16)

    def rows_of(chip_shift, flip):
        who = lax.rem(lax.div(d, 2) + 16 - chip_shift, 16) * 2 + lax.rem(d + flip, 2)
        return brick.at[:, pl.ds(pl.multiple_of(who * PIECE, PIECE), PIECE), :]

    @pl.when(jnp.logical_not(here))
    def _():
        remote(rows_of(0, 0), rows_of(0, 0), piece_send.at[0], piece_recv, (z, d)).wait_recv()

    def go(shift):
        return remote(rows_of(0, 0), rows_of(0, 0), go_send.at[shift], go_recv.at[shift], (z, at_chip(d, shift)))

    def came(shift):
        return remote(rows_of(shift, 0), rows_of(shift, 0), go_send.at[shift], go_recv.at[shift], (z, d))

    def across(shift):
        return remote(rows_of(shift, 0), rows_of(shift, 0), twin_send.at[shift], twin_recv.at[shift], (z, twin(d)))

    def from_twin(shift):
        return remote(rows_of(shift, 1), rows_of(shift, 1), twin_send.at[shift], twin_recv.at[shift], (z, twin(d)))

    @pl.loop(1, 16)
    def _(shift):
        go(shift).start()

    across(0).start()

    @pl.loop(1, 16)
    def _(shift):
        came(shift).wait_recv()
        across(shift).start()

    @pl.loop(0, 16)
    def _(shift):
        from_twin(shift).wait_recv()

    @pl.loop(1, 16)
    def _(shift):
        go(shift).wait_send()

    @pl.loop(0, 16)
    def _(shift):
        across(shift).wait_send()


def strips(k, source, dest, sems):
    return [
        pltpu.make_async_copy(
            source.at[:, pl.ds(pl.multiple_of((K * j + k) * STRIP, STRIP), STRIP)],
            dest.at[:, pl.ds(j * STRIP, STRIP)],
            sems.at[j],
        )
        for j in range(FQ)
    ]


def hidden_kernel(pick, ids, gates, tokens, cotangent, brick, act, tok, cot, part, got, tok_sem, cot_sem, part_send, part_recv, act_send, act_recv):
    z, d, f, k = place()
    barrier = pltpu.get_barrier_semaphore()

    def peer(shift):
        return f * K + lax.rem(k + shift, K)

    for shift in range(1, K):
        greet(barrier, (peer(shift), d))
    loads = strips(k, tokens, tok, tok_sem) + strips(k, cotangent, cot, cot_sem)
    for copy in loads:
        copy.start()
    for copy in loads:
        copy.wait()
    for m, left in enumerate((tok, tok, cot)):
        part[:, m] = nn(left[...], brick[m]).astype(BF).reshape(K, 32, HQ)
    pl.semaphore_wait(barrier, K - 1)

    def give(shift):
        to = lax.rem(k + shift, K)
        return remote(part.at[to], got.at[shift], part_send.at[shift], part_recv.at[shift], (peer(shift), d))

    for shift in range(1, K):
        give(shift).start()
    got[0] = part[k]
    rows = pl.ds(pl.multiple_of(k * 32, 32), 32)
    matched = jnp.where(ids[rows, :] == pick[0], gates[rows, :].astype(F32), 0.0)
    weight = jnp.sum(matched, axis=1, keepdims=True) / 65536.0
    for shift in range(1, K):
        give(shift).wait_recv()
    total = got[0].astype(F32)
    for shift in range(1, K):
        total = total + got[shift].astype(F32)
    gate, up, back = total[0], total[1], total[2]
    s = jax.nn.sigmoid(gate)
    active = gate * s
    act[k, 0] = (weight * active * up).astype(BF)
    act[k, 1] = (weight * back * up * s * (1.0 + gate * (1.0 - s))).astype(BF)
    act[k, 2] = (weight * back * active).astype(BF)

    def show(shift):
        return remote(act.at[k], act.at[k], act_send.at[shift], act_recv.at[shift], (peer(shift), d))

    def shown(shift):
        who = lax.rem(k + K - shift, K)
        return remote(act.at[who], act.at[who], act_send.at[shift], act_recv.at[shift], (peer(shift), d))

    for shift in range(1, K):
        show(shift).start()
    for shift in range(1, K):
        shown(shift).wait_recv()
    for shift in range(1, K):
        give(shift).wait_send()
        show(shift).wait_send()


def out_kernel(z0, tokens, cotangent, brick, act, moe, dx, grads, tok, cot, part, got, product, half, middle, inbox, piece, tok_sem, cot_sem, part_send, part_recv, swap_send, swap_recv, go_send, go_recv, home_send, home_recv):
    z, d, f, k = place()
    f0, k0 = z0 // K, z0 % K
    here = jnp.logical_and(z == z0, lax.rem(d, K) == k0)
    away = jnp.logical_not(here)
    barrier = pltpu.get_barrier_semaphore()
    greet_plane(barrier, z, d)

    def lane(shift):
        return lax.rem(f + shift, FQ) * K + k

    for shift in range(1, FQ):
        greet(barrier, (lane(shift), d))

    def origin(i):
        return lax.div(i, K) * K + lax.rem(d, K), lax.div(d, K) * K + lax.rem(i, K)

    def remote_origin(i):
        from_z, from_d = origin(i)
        return jnp.logical_or(from_z != z, from_d != d)

    @pl.when(z == z0)
    def _():
        @pl.loop(0, 32)
        def _(i):
            @pl.when(remote_origin(i))
            def _():
                greet(barrier, origin(i))

    loads = strips(k, tokens, tok, tok_sem) + strips(k, cotangent, cot, cot_sem)
    for copy in loads:
        copy.start()

    @pl.when(z != z0)
    def _():
        grads[...] = jnp.zeros_like(grads)

    hidden = act[:, 0].reshape(256, HQ)
    d_gate = act[:, 1].reshape(256, HQ)
    d_up = act[:, 2].reshape(256, HQ)
    for j in range(FQ):
        rows = slice(j * STRIP, (j + 1) * STRIP)
        part[j, 0] = nt(hidden, brick[2, rows, :]).astype(BF)
        part[j, 1] = (nt(d_gate, brick[0, rows, :]) + nt(d_up, brick[1, rows, :])).astype(BF)
    for copy in loads:
        copy.wait()
    for m, (left, right) in enumerate(((tok, d_gate), (tok, d_up), (cot, hidden))):
        value = tn(left[...], right).astype(BF).reshape(16, 2, PIECE, HQ)
        product[0, :, m] = value[:, 0]
        product[1, :, m] = value[:, 1]

    @pl.when(here)
    def _():
        pl.semaphore_wait(barrier, 16 + FQ - 1)

    @pl.when(away)
    def _():
        pl.semaphore_wait(barrier, 16 + FQ)

    core, chip = lax.rem(d, 2), lax.div(d, 2)
    swap = remote(product.at[1 - core], half, swap_send, swap_recv, (z, twin(d)))
    swap.start()

    def give(shift):
        return remote(
            part.at[lax.rem(f + shift, FQ)], got.at[shift], part_send.at[shift], part_recv.at[shift], (lane(shift), d)
        )

    for shift in range(1, FQ):
        give(shift).start()
    swap.wait_recv()
    middle[...] = (product[core].astype(F32) + half[...].astype(F32)).astype(BF)

    def go(shift):
        return remote(
            middle.at[lax.rem(chip + shift, 16)], inbox.at[shift], go_send.at[shift], go_recv.at[shift], (z, at_chip(d, shift))
        )

    @pl.loop(1, 16)
    def _(shift):
        go(shift).start()

    inbox[0] = middle[chip]

    @pl.loop(1, 16)
    def _(shift):
        go(shift).wait_recv()

    total = inbox[0].astype(F32)
    for shift in range(1, 16):
        total = total + inbox[shift].astype(F32)
    piece[...] = total.astype(BF)

    def spot(from_f, from_p):
        rows = pl.ds(pl.multiple_of(from_p * PIECE, PIECE), PIECE)
        cols = pl.ds(pl.multiple_of(from_f * HQ, HQ), HQ)
        return grads.at[:, rows, cols]

    number = f * K + lax.rem(d, K)
    home = remote(
        piece, spot(f, lax.rem(d, K)), home_send, home_recv.at[number], (z0, lax.div(d, K) * K + k)
    )

    @pl.when(away)
    def _():
        home.start()

    @pl.when(here)
    def _():
        own = pltpu.make_async_copy(piece, spot(f, lax.rem(d, K)), home_send)
        own.start()
        own.wait()

    for shift in range(1, FQ):
        give(shift).wait_recv()
    result = part[f].astype(F32)
    for shift in range(1, FQ):
        result = result + got[shift].astype(F32)
    moe[...] = result[0].astype(BF)
    dx[...] = result[1].astype(BF)

    @pl.when(z == z0)
    def _():
        @pl.loop(0, 32)
        def _(i):
            @pl.when(remote_origin(i))
            def _():
                where = spot(lax.div(i, K), lax.rem(i, K))
                remote(where, where, home_send, home_recv.at[i], (z, d)).wait_recv()

    swap.wait_send()
    for shift in range(1, FQ):
        give(shift).wait_send()

    @pl.loop(1, 16)
    def _(shift):
        go(shift).wait_send()

    @pl.when(away)
    def _():
        home.wait_send()


def params(number):
    return pltpu.CompilerParams(collective_id=number, has_side_effects=True, vmem_limit_bytes=LIMIT)


def dma(*shape):
    return pltpu.SemaphoreType.DMA(shape)


def pull(z0, pick, wg, wu, wd):
    return pl.pallas_call(
        functools.partial(pull_kernel, z0),
        out_shape=jax.ShapeDtypeStruct((3, WIDTH, HQ), BF),
        in_specs=[SM, HBM, HBM, HBM],
        out_specs=VM,
        scratch_shapes=[
            pltpu.VMEM((3, 2, STRIP, 1024), BF),
            pltpu.VMEM((3, STRIP, 1024), BF),
            dma(4),
            dma(32),
            pltpu.SemaphoreType.DMA,
            dma(16),
            dma(16),
            dma(16),
            dma(16),
        ],
        compiler_params=params(1 + z0),
        name=f"pull_{z0}",
    )(pick, wg, wu, wd)


def hidden_part(pick, ids, gates, tokens, cotangent, brick):
    return pl.pallas_call(
        hidden_kernel,
        out_shape=jax.ShapeDtypeStruct((K, 3, 32, HQ), BF),
        in_specs=[SM, VM, VM, HBM, HBM, VM],
        out_specs=VM,
        scratch_shapes=[
            pltpu.VMEM((256, WIDTH), BF),
            pltpu.VMEM((256, WIDTH), BF),
            pltpu.VMEM((K, 3, 32, HQ), BF),
            pltpu.VMEM((K, 3, 32, HQ), BF),
            dma(FQ),
            dma(FQ),
            dma(K),
            dma(K),
            dma(K),
            dma(K),
        ],
        compiler_params=params(40),
        name="hidden",
    )(pick, ids, gates, tokens, cotangent, brick)


def finish(z0, tokens, cotangent, brick, act):
    return pl.pallas_call(
        functools.partial(out_kernel, z0),
        out_shape=(
            jax.ShapeDtypeStruct((256, STRIP), BF),
            jax.ShapeDtypeStruct((256, STRIP), BF),
            jax.ShapeDtypeStruct((3, STRIP, 1024), BF),
        ),
        in_specs=[HBM, HBM, VM, VM],
        out_specs=(VM, VM, VM),
        scratch_shapes=[
            pltpu.VMEM((256, WIDTH), BF),
            pltpu.VMEM((256, WIDTH), BF),
            pltpu.VMEM((FQ, 2, 256, STRIP), BF),
            pltpu.VMEM((FQ, 2, 256, STRIP), BF),
            pltpu.VMEM((2, 16, 3, PIECE, HQ), BF),
            pltpu.VMEM((16, 3, PIECE, HQ), BF),
            pltpu.VMEM((16, 3, PIECE, HQ), BF),
            pltpu.VMEM((16, 3, PIECE, HQ), BF),
            pltpu.VMEM((3, PIECE, HQ), BF),
            dma(FQ),
            dma(FQ),
            dma(FQ),
            dma(FQ),
            pltpu.SemaphoreType.DMA,
            pltpu.SemaphoreType.DMA,
            dma(16),
            dma(16),
            pltpu.SemaphoreType.DMA,
            dma(32),
        ],
        compiler_params=params(41 + z0),
        name=f"finish_{z0}",
    )(tokens, cotangent, brick, act)


def per_device(tokens, out_grad, expert_ids, gate_fixed, expert_pick, w_gate, w_up, w_down):
    picked = expert_pick[0]
    owner = picked // 2
    brick = lax.switch(
        owner, [functools.partial(pull, z0) for z0 in range(NZ)], expert_pick, w_gate, w_up, w_down
    )
    act = hidden_part(expert_pick, expert_ids, gate_fixed, tokens, out_grad, brick)
    moe, dx, grads = lax.switch(
        owner, [functools.partial(finish, z0) for z0 in range(NZ)], tokens, out_grad, brick, act
    )
    is_owner = lax.axis_index("expert") == owner
    kept = jnp.logical_and(jnp.arange(2) == picked % 2, is_owner)[:, None, None]
    zero = jnp.zeros((), BF)
    return (moe, dx) + tuple(jnp.where(kept, grads[m][None], zero) for m in range(3))


def solution(mesh):
    rows = P("dp", None)
    owned = P("expert", "dp", None)
    return jax.shard_map(
        per_device,
        mesh=mesh,
        in_specs=(rows, rows, rows, rows, P(), owned, owned, owned),
        out_specs=(P("dp", "expert"), P("dp", "expert"), owned, owned, owned),
        check_vma=False,
    )
```

```python
import functools

import jax
import jax.numpy as jnp
from jax import lax
from jax.experimental import pallas as pl
from jax.experimental.pallas import tpu as pltpu
from jax.sharding import PartitionSpec as P

NZ, ND = 32, 32
K, FQ = 8, 4
STRIP, HQ, PIECE = 128, 256, 16
WIDTH = FQ * STRIP
MESH = pl.DeviceIdType.MESH
BF = jnp.bfloat16
F32 = jnp.float32
LIMIT = 48 << 20
VM = pl.BlockSpec(memory_space=pltpu.VMEM)
HBM = pl.BlockSpec(memory_space=pl.ANY)
SM = pl.BlockSpec(memory_space=pltpu.SMEM)


def place():
    z = lax.axis_index("expert")
    d = lax.axis_index("dp")
    return z, d, lax.div(z, K), lax.rem(z, K)


def greet(barrier, device):
    pl.semaphore_signal(barrier, inc=1, device_id=device, device_id_type=MESH)


def remote(src, dst, send, recv, device):
    return pltpu.make_async_remote_copy(
        src_ref=src, dst_ref=dst, send_sem=send, recv_sem=recv, device_id=device, device_id_type=MESH
    )


def at_chip(d, shift):
    chip, core = lax.div(d, 2), lax.rem(d, 2)
    return lax.rem(chip + shift, 16) * 2 + core


def twin(d):
    return d + 1 - 2 * lax.rem(d, 2)


def greet_plane(barrier, z, d):
    @pl.loop(1, 16)
    def _(shift):
        greet(barrier, (z, at_chip(d, shift)))

    greet(barrier, (z, twin(d)))


def nn(a, b):
    return jnp.dot(a, b, preferred_element_type=F32)


def nt(a, b):
    return lax.dot_general(a, b, (((1,), (1,)), ((), ())), preferred_element_type=F32)


def tn(a, b):
    return lax.dot_general(a, b, (((0,), (0,)), ((), ())), preferred_element_type=F32)


def strips(k, source, dest, sems):
    return [
        pltpu.make_async_copy(
            source.at[:, pl.ds(pl.multiple_of((K * j + k) * STRIP, STRIP), STRIP)],
            dest.at[:, pl.ds(j * STRIP, STRIP)],
            sems.at[j],
        )
        for j in range(FQ)
    ]


def layer_kernel(pair, pick, ids, gates, tokens, cotangent, wg, wu, wd, moe, dx, grads, both, stage, letter, brick, tok, cot, tpart, tgot, act, part, got, product, half, middle, inbox, piece, load, tok_sem, cot_sem, piece_send, piece_recv, go_send, go_recv, twin_send, twin_recv, tpart_send, tpart_recv, act_send, act_recv, part_send, part_recv, swap_send, swap_recv, out_send, out_recv, home_send, home_recv):
    z, d, f, k = place()
    parity = lax.rem(z, 2)
    source = lax.div(d, K) * K + k
    owns = lax.div(z, 2) == pair
    here = jnp.logical_and(owns, source == d)
    barrier = pltpu.get_barrier_semaphore()

    def peer(shift):
        return f * K + lax.rem(k + shift, K)

    def lane(shift):
        return lax.rem(f + shift, FQ) * K + k

    def target(i):
        return lax.div(i, K) * K + lax.rem(d, K), lax.div(d, K) * K + lax.rem(i, K)

    def away(i):
        to_z, to_d = target(i)
        return jnp.logical_or(to_z != z, to_d != d)

    def not_me(side):
        return jnp.logical_or(2 * pair + side != z, source != d)

    for side in range(2):
        @pl.when(not_me(side))
        def _():
            greet(barrier, (2 * pair + side, source))

    @pl.when(owns)
    def _():
        @pl.loop(0, 32)
        def _(i):
            @pl.when(away(i))
            def _():
                greet(barrier, target(i))

    greet_plane(barrier, z, d)
    for shift in range(1, K):
        greet(barrier, (peer(shift), d))
    for shift in range(1, FQ):
        greet(barrier, (lane(shift), d))

    loads = strips(k, tokens, tok, tok_sem) + strips(k, cotangent, cot, cot_sem)
    for copy in loads:
        copy.start()
    rows = pl.ds(pl.multiple_of(k * 32, 32), 32)
    matched = jnp.where(ids[rows, :] == pick[0], gates[rows, :].astype(F32), 0.0)
    weight = jnp.sum(matched, axis=1, keepdims=True) / 65536.0

    @pl.when(jnp.logical_not(owns))
    def _():
        grads[...] = jnp.zeros_like(grads)

    @pl.when(owns)
    def _():
        fetch = [pltpu.make_async_copy(w, both.at[m], load.at[m]) for m, w in enumerate((wg, wu, wd))]
        for copy in fetch:
            copy.start()
        for copy in fetch:
            copy.wait()
        slot = lax.rem(pick[0], 2)
        for m in range(3):
            stage[m] = jnp.where(slot == 0, both[m, 0], both[m, 1])

    for copy in loads:
        copy.wait()

    @pl.when(jnp.logical_not(owns))
    def _():
        pl.semaphore_wait(barrier, 28)

    @pl.when(jnp.logical_and(owns, source != d))
    def _():
        pl.semaphore_wait(barrier, 60)

    @pl.when(here)
    def _():
        pl.semaphore_wait(barrier, 58)

    def cut(i):
        at = pl.ds(pl.multiple_of(lax.rem(i, K) * PIECE, PIECE), PIECE)
        cols = pl.ds(pl.multiple_of(lax.div(i, K) * HQ, HQ), HQ)
        return stage.at[:, at, cols]

    def spot(i):
        at = pl.ds(pl.multiple_of(lax.rem(i, K) * PIECE, PIECE), PIECE)
        cols = pl.ds(pl.multiple_of(lax.div(i, K) * HQ, HQ), HQ)
        return grads.at[:, at, cols]

    def hand(i):
        return remote(cut(i), letter.at[parity], piece_send.at[i], piece_recv.at[parity], target(i))

    number = f * K + lax.rem(d, K)

    @pl.when(owns)
    def _():
        @pl.loop(0, 32)
        def _(i):
            @pl.when(away(i))
            def _():
                hand(i).start()

        @pl.when(here)
        def _():
            own = pltpu.make_async_copy(cut(number), letter.at[parity], load.at[3])
            own.start()
            own.wait()

    for side in range(2):
        @pl.when(not_me(side))
        def _():
            remote(letter.at[side], letter.at[side], piece_send.at[0], piece_recv.at[side], (z, d)).wait_recv()

    side_now = lax.rem(lax.div(pick[0], 2), 2)
    mine = pl.ds(pl.multiple_of(d * PIECE, PIECE), PIECE)
    brick[:, mine, :] = jnp.where(side_now == 0, letter[0], letter[1])

    def rows_of(chip_shift, flip):
        who = lax.rem(lax.div(d, 2) + 16 - chip_shift, 16) * 2 + lax.rem(d + flip, 2)
        return brick.at[:, pl.ds(pl.multiple_of(who * PIECE, PIECE), PIECE), :]

    def go(shift):
        return remote(rows_of(0, 0), rows_of(0, 0), go_send.at[shift], go_recv.at[shift], (z, at_chip(d, shift)))

    def came(shift):
        return remote(rows_of(shift, 0), rows_of(shift, 0), go_send.at[shift], go_recv.at[shift], (z, d))

    def across(shift):
        return remote(rows_of(shift, 0), rows_of(shift, 0), twin_send.at[shift], twin_recv.at[shift], (z, twin(d)))

    def from_twin(shift):
        return remote(rows_of(shift, 1), rows_of(shift, 1), twin_send.at[shift], twin_recv.at[shift], (z, twin(d)))

    @pl.loop(1, 16)
    def _(shift):
        go(shift).start()

    across(0).start()

    @pl.loop(1, 16)
    def _(shift):
        came(shift).wait_recv()
        across(shift).start()

    @pl.loop(0, 16)
    def _(shift):
        from_twin(shift).wait_recv()

    for m, left in enumerate((tok, tok, cot)):
        tpart[:, m] = nn(left[...], brick[m]).astype(BF).reshape(K, 32, HQ)

    def tgive(shift):
        to = lax.rem(k + shift, K)
        return remote(tpart.at[to], tgot.at[shift], tpart_send.at[shift], tpart_recv.at[shift], (peer(shift), d))

    for shift in range(1, K):
        tgive(shift).start()
    tgot[0] = tpart[k]
    for shift in range(1, K):
        tgive(shift).wait_recv()
    total = tgot[0].astype(F32)
    for shift in range(1, K):
        total = total + tgot[shift].astype(F32)
    gate, up, back = total[0], total[1], total[2]
    s = jax.nn.sigmoid(gate)
    active = gate * s
    act[k, 0] = (weight * active * up).astype(BF)
    act[k, 1] = (weight * back * up * s * (1.0 + gate * (1.0 - s))).astype(BF)
    act[k, 2] = (weight * back * active).astype(BF)

    def show(shift):
        return remote(act.at[k], act.at[k], act_send.at[shift], act_recv.at[shift], (peer(shift), d))

    def shown(shift):
        who = lax.rem(k + K - shift, K)
        return remote(act.at[who], act.at[who], act_send.at[shift], act_recv.at[shift], (peer(shift), d))

    for shift in range(1, K):
        show(shift).start()
    for shift in range(1, K):
        shown(shift).wait_recv()

    hidden = act[:, 0].reshape(256, HQ)
    d_gate = act[:, 1].reshape(256, HQ)
    d_up = act[:, 2].reshape(256, HQ)
    for j in range(FQ):
        strip = slice(j * STRIP, (j + 1) * STRIP)
        part[j, 0] = nt(hidden, brick[2, strip, :]).astype(BF)
        part[j, 1] = (nt(d_gate, brick[0, strip, :]) + nt(d_up, brick[1, strip, :])).astype(BF)

    def give(shift):
        return remote(
            part.at[lax.rem(f + shift, FQ)], got.at[shift], part_send.at[shift], part_recv.at[shift], (lane(shift), d)
        )

    for shift in range(1, FQ):
        give(shift).start()
    for m, (left, right) in enumerate(((tok, d_gate), (tok, d_up), (cot, hidden))):
        value = tn(left[...], right).astype(BF).reshape(16, 2, PIECE, HQ)
        product[0, :, m] = value[:, 0]
        product[1, :, m] = value[:, 1]

    core, chip = lax.rem(d, 2), lax.div(d, 2)
    swap = remote(product.at[1 - core], half, swap_send, swap_recv, (z, twin(d)))
    swap.start()
    swap.wait_recv()
    middle[...] = (product[core].astype(F32) + half[...].astype(F32)).astype(BF)

    def out(shift):
        return remote(
            middle.at[lax.rem(chip + shift, 16)], inbox.at[shift], out_send.at[shift], out_recv.at[shift], (z, at_chip(d, shift))
        )

    @pl.loop(1, 16)
    def _(shift):
        out(shift).start()

    inbox[0] = middle[chip]

    @pl.loop(1, 16)
    def _(shift):
        out(shift).wait_recv()

    summed = inbox[0].astype(F32)
    for shift in range(1, 16):
        summed = summed + inbox[shift].astype(F32)
    piece[...] = summed.astype(BF)

    def home(side):
        return remote(piece, spot(number), home_send.at[side], home_recv.at[number], (2 * pair + side, source))

    for side in range(2):
        @pl.when(not_me(side))
        def _():
            home(side).start()

    @pl.when(here)
    def _():
        own = pltpu.make_async_copy(piece, spot(number), load.at[3])
        own.start()
        own.wait()

    for shift in range(1, FQ):
        give(shift).wait_recv()
    result = part[f].astype(F32)
    for shift in range(1, FQ):
        result = result + got[shift].astype(F32)
    moe[...] = result[0].astype(BF)
    dx[...] = result[1].astype(BF)

    @pl.when(owns)
    def _():
        @pl.loop(0, 32)
        def _(i):
            @pl.when(away(i))
            def _():
                remote(spot(i), spot(i), home_send.at[0], home_recv.at[i], (z, d)).wait_recv()
                hand(i).wait_send()

    @pl.loop(1, 16)
    def _(shift):
        go(shift).wait_send()
        out(shift).wait_send()

    @pl.loop(0, 16)
    def _(shift):
        across(shift).wait_send()

    for shift in range(1, K):
        tgive(shift).wait_send()
        show(shift).wait_send()
    swap.wait_send()
    for shift in range(1, FQ):
        give(shift).wait_send()
    for side in range(2):
        @pl.when(not_me(side))
        def _():
            home(side).wait_send()


def dma(*shape):
    return pltpu.SemaphoreType.DMA(shape)


def buffer(*shape):
    return pltpu.VMEM(shape, BF)


def layer(pair, *operands):
    return pl.pallas_call(
        functools.partial(layer_kernel, pair),
        out_shape=(
            jax.ShapeDtypeStruct((256, STRIP), BF),
            jax.ShapeDtypeStruct((256, STRIP), BF),
            jax.ShapeDtypeStruct((3, STRIP, 1024), BF),
        ),
        in_specs=[SM, VM, VM, HBM, HBM, HBM, HBM, HBM],
        out_specs=(VM, VM, VM),
        scratch_shapes=[
            buffer(3, 2, STRIP, 1024),
            buffer(3, STRIP, 1024),
            buffer(2, 3, PIECE, HQ),
            buffer(3, WIDTH, HQ),
            buffer(256, WIDTH),
            buffer(256, WIDTH),
            buffer(K, 3, 32, HQ),
            buffer(K, 3, 32, HQ),
            buffer(K, 3, 32, HQ),
            buffer(FQ, 2, 256, STRIP),
            buffer(FQ, 2, 256, STRIP),
            buffer(2, 16, 3, PIECE, HQ),
            buffer(16, 3, PIECE, HQ),
            buffer(16, 3, PIECE, HQ),
            buffer(16, 3, PIECE, HQ),
            buffer(3, PIECE, HQ),
            dma(4), dma(FQ), dma(FQ), dma(32), dma(2),
            dma(16), dma(16), dma(16), dma(16),
            dma(K), dma(K), dma(K), dma(K), dma(FQ), dma(FQ),
            pltpu.SemaphoreType.DMA, pltpu.SemaphoreType.DMA,
            dma(16), dma(16), dma(2), dma(32),
        ],
        compiler_params=pltpu.CompilerParams(
            collective_id=1 + pair, has_side_effects=True, vmem_limit_bytes=LIMIT
        ),
        name=f"layer_{pair}",
    )(*operands)


def per_device(tokens, out_grad, expert_ids, gate_fixed, expert_pick, w_gate, w_up, w_down):
    picked = expert_pick[0]
    owner = picked // 2
    moe, dx, grads = lax.switch(
        owner // 2,
        [functools.partial(layer, pair) for pair in range(NZ // 2)],
        expert_pick, expert_ids, gate_fixed, tokens, out_grad, w_gate, w_up, w_down,
    )
    is_owner = lax.axis_index("expert") == owner
    kept = jnp.logical_and(jnp.arange(2) == picked % 2, is_owner)[:, None, None]
    zero = jnp.zeros((), BF)
    return (moe, dx) + tuple(jnp.where(kept, grads[m][None], zero) for m in range(3))


def solution(mesh):
    rows = P("dp", None)
    owned = P("expert", "dp", None)
    return jax.shard_map(
        per_device,
        mesh=mesh,
        in_specs=(rows, rows, rows, rows, P(), owned, owned, owned),
        out_specs=(P("dp", "expert"), P("dp", "expert"), owned, owned, owned),
        check_vma=False,
    )
```
